32 devices in a mesh: parts: 2 (over x), mp: 16 (over z, y, core).
Axes of the slice: x: 2, y: 2, z: 4, core: 2. Of those that a mesh axis runs over, the one named last changes fastest.
Arguments:
- probes: float32 [32, 262144], P(None, ('parts', 'mp')), parts along dimension 1, may hold values from -6 to 6
- illumination: float32 [4, 262144], P(None, ('parts', 'mp')), parts along dimension 1, may hold values from 1 to 90, as said below
- damping: float32 [262144], P(('parts', 'mp')), parts along dimension 0, may hold values from 0.5 to 2
- wavelets: float32 [8, 513], P('parts'), parts along dimension 0, may hold values from -0.25 to 0.25
Outputs:
- basis: float32 [32, 262144], P(None, ('parts', 'mp')), parts along dimension 1
- r_factor: float32 [64, 32], P('parts'), parts along dimension 0
The draws below stay inside these ranges and needn't reach their ends.
There are 2 independent parts, one for each index of `parts`. The reference program is written for one: setup_inputs(seed, part) draws one part's arguments, and reference() takes and returns one part's arrays. A program takes and returns all parts, laid end to end along the dimension named above; each array names one. Nothing has to cross between parts.
Inputs may be any that keep to these rules, and one draw needn't show every extreme that they name: `illumination`: positive data weights.
All inputs are finite; a program needn't handle non-finite values.
Results may differ from the reference program's by a relative error of at most 0.0001.
Values sent between devices are 32-bit elements; how exact they have to be, the bound alone decides.
A program may use at most 64 MiB of HBM per device.

```python
import math
import jax
import jax.numpy as jnp
from jax import lax

P_SIZE = 32
W = 256
S = 4
M = 131072


def draw_illumination(key, part):
    key = jax.random.fold_in(key, 7)
    position = jnp.arange(M, dtype=jnp.float32)[None, :] / M
    rough = jnp.exp(jax.random.uniform(key, (S, M), jnp.float32, 0.0, jnp.log(10.0)))
    return rough * jnp.exp(jnp.log(3.0) * position)


def block_levels(own_key, shape, pieces, least, high):
    level = 1.0
    for dim, blocks in pieces:
        steps = jax.random.uniform(jax.random.fold_in(jax.random.fold_in(own_key, 6), dim), (blocks,), jnp.float32, least / len(pieces), high / len(pieces))
        level = level * jnp.repeat(jnp.exp(steps), shape[dim] // blocks).reshape((-1,) + (1,) * (len(shape) - 1 - dim))
    return level


def scatter_about(key, shape, width, most, split=(), kind=jnp.bfloat16):
    gain = block_levels(key, shape, split, -0.22, 0.18) if split else 1.0
    entries = jax.random.normal(key, shape, jnp.float32) * width * gain
    return jnp.minimum(jnp.maximum(entries, -most), most).astype(kind)


def setup_inputs(seed: int = 0, part: int = 0) -> dict:
    key_of = jax.random.split(jax.random.key(seed), 5)
    part_keys = jax.random.split(jax.random.fold_in(key_of[4], part), 5)
    probes = scatter_about(part_keys[0], (P_SIZE, M), 1.0, 6.0, ((1, 16),), jnp.float32)
    illumination = draw_illumination(jax.random.fold_in(jax.random.fold_in(key_of[4], part), 71), part)
    damping = jnp.clip(jnp.exp(math.log(2.0) - 1.3862944 * jax.random.uniform(part_keys[2], (M,), jnp.float32) ** block_levels(part_keys[2], (M,), ((0, 16),), -0.2, 0.2)), 0.5, 2.0)
    wavelets = scatter_about(part_keys[3], (S, 2 * W + 1), (2 * W + 1) ** -0.5, 0.25, (), jnp.float32)
    return {"probes": probes, "illumination": illumination, "damping": damping, "wavelets": wavelets}


def hessian(vectors, illumination, damping, wavelets):
    length = 2 * M
    spectrum = jnp.fft.rfft(vectors, n=length, axis=1)

    def one_shot(summed, inputs):
        wavelet, weight = inputs
        forward = jnp.fft.irfft(spectrum * jnp.fft.rfft(wavelet, n=length), n=length, axis=1)[:, W:W + M]
        response = forward * weight[None, :]
        reflected = jnp.fft.rfft(response, n=length, axis=1) * jnp.fft.rfft(wavelet[::-1], n=length)
        backward = jnp.fft.irfft(reflected, n=length, axis=1)[:, W:W + M]
        return (summed + backward, None)
    summed, _ = lax.scan(one_shot, jnp.zeros((P_SIZE, M), jnp.float32), (wavelets, illumination))
    return summed / S + damping[None, :] * vectors

def orthonormal(images):
    gramian = jnp.dot(images, images.T, precision=lax.Precision.HIGHEST) / M
    factor_low = jnp.linalg.cholesky(gramian)
    identity = jnp.eye(P_SIZE, dtype=jnp.float32)
    inverse = lax.linalg.triangular_solve(factor_low, identity, left_side=True, lower=True)
    return (jnp.dot(inverse, images, precision=lax.Precision.HIGHEST), factor_low)

def reference(probes, illumination, damping, wavelets):
    first_basis, _ = orthonormal(hessian(probes, illumination, damping, wavelets))
    basis, factor_low = orthonormal(hessian(first_basis, illumination, damping, wavelets))
    return (basis, factor_low)
```

```python
import functools

import jax
import jax.numpy as jnp
from jax import lax
from jax.experimental import pallas as pl
from jax.experimental.pallas import tpu as pltpu
from jax.sharding import PartitionSpec as P

W = 256
LANES = 128
MESH = pl.DeviceIdType.MESH
F32 = jnp.float32
BF16 = jnp.bfloat16
EXACT = lax.Precision.HIGHEST


def split(value):
    high = value.astype(BF16)
    return high, (value - high.astype(F32)).astype(BF16)


def iota(shape, dim):
    return lax.broadcasted_iota(jnp.int32, shape, dim)


def store_band(taps, last, high_ref, low_ref, shot):
    top = pltpu.roll(
        jnp.broadcast_to(taps, (LANES, 2 * W)), 0, 1, stride=1, stride_axis=0
    )
    bottom = jnp.concatenate([top[:, 2 * W - LANES :], top[:, : 2 * W - LANES]], axis=1)
    turned = jnp.concatenate([top, bottom], axis=0)
    edge = turned[:, :W]
    row, col = iota((W, W), 0), iota((W, W), 1)
    first = jnp.where(col < row, edge, jnp.where(col == row, last, 0.0))
    third = jnp.where(col >= row, edge, 0.0)
    for offset, tile in enumerate((first, turned[:, W:], third)):
        high, low = split(tile)
        rows = slice(offset * W, (offset + 1) * W)
        high_ref[shot, rows, :] = high
        low_ref[shot, rows, :] = low


def gram_of(high_ref, low_ref, start, block_count, rows):
    group = 8 * rows
    total = None
    for g in range(block_count // 8):
        at = slice(start + g * group, start + (g + 1) * group)
        high, low = high_ref[at, :], low_ref[at, :]
        left = jnp.concatenate([high, high, low], axis=1)
        right = jnp.concatenate([high, low, high], axis=1)
        term = lax.dot_general(
            left, right, (((1,), (1,)), ((), ())), preferred_element_type=F32
        )
        total = term if total is None else total + term
    same = iota((group, group), 0) // rows == iota((group, group), 1) // rows
    total = jnp.where(same, total, 0.0)
    folded = total[:rows]
    for i in range(1, 8):
        folded = folded + total[i * rows : (i + 1) * rows]
    folded = folded[:, :LANES] + folded[:, LANES:]
    folded = folded + pltpu.roll(folded, 64, 1)
    folded = folded + pltpu.roll(folded, 32, 1)
    lane = iota((8, LANES), 1) // 32
    packed = folded[:8]
    for i in range(1, 4):
        packed = jnp.where(lane == i, folded[8 * i : 8 * i + 8], packed)
    return packed


def unpack(packed):
    slabs = [packed] + [pltpu.roll(packed, LANES - 32 * i, 1) for i in range(1, 4)]
    return jnp.concatenate(slabs, axis=0)


def factor(gram, rows):
    row, lane = iota((rows, LANES), 0), iota((rows, LANES), 1)
    work = jnp.where(lane < rows, gram, jnp.where(lane == row + rows, 1.0, 0.0))
    unit = jnp.zeros((rows, LANES), F32)
    for k in range(rows):
        pivot_row = work[k : k + 1, :]
        ratio = work[:, k : k + 1] * (1.0 / work[k : k + 1, k : k + 1])
        unit = jnp.where((lane == k) & (row >= k), ratio, unit)
        work = work - jnp.where(row > k, ratio, 0.0) * pivot_row
    diagonal = jnp.where(lane == row, work, 0.0)
    down = jnp.sum(diagonal, axis=1, keepdims=True)
    along = jnp.sum(diagonal, axis=0, keepdims=True)
    lower = unit * jnp.sqrt(along)
    inverse = pltpu.roll(work, LANES - rows, 1) / jnp.sqrt(down)
    return lower[:, :rows], inverse[:, :rows]


def forward_stage(count, chunks, rows, src, weights, dst, light_ref, light_at, shots):
    step = count // chunks
    size = step * rows

    def chunk(c, carry):
        start = c * step
        at = pl.multiple_of(start * rows, rows)
        highs = [src[0][pl.ds(at + o * rows, size), :] for o in range(3)]
        lows = [src[1][pl.ds(at + o * rows, size), :] for o in range(3)]
        left = jnp.concatenate(highs + lows + highs, axis=1)
        for s in range(shots):
            wh, wl = weights[0][s], weights[1][s]
            right = jnp.concatenate([wh, wh, wl], axis=0)
            acc = jnp.dot(left, right, preferred_element_type=F32)
            light = jnp.concatenate(
                [
                    jnp.broadcast_to(light_ref[start + light_at + j, s : s + 1, :], (rows, W))
                    for j in range(step)
                ],
                axis=0,
            )
            high, low = split(acc * light)
            dst[0][s, pl.ds(at, size), :] = high
            dst[1][s, pl.ds(at, size), :] = low
        return carry

    lax.fori_loop(0, chunks, chunk, 0)


def adjoint_stage(count, chunks, rows, src, weights, dst, same, damp_ref, damp_at, shots):
    step = count // chunks
    size = step * rows

    def chunk(c, carry):
        start = c * step
        at = pl.multiple_of(start * rows, rows)
        acc = None
        for s in range(shots):
            highs = [src[0][s, pl.ds(at + o * rows, size), :] for o in range(3)]
            lows = [src[1][s, pl.ds(at + o * rows, size), :] for o in range(3)]
            wh, wl = weights[0][s], weights[1][s]
            left = jnp.concatenate(highs + lows + highs, axis=1)
            right = jnp.concatenate([wh, wh, wl], axis=0)
            term = jnp.dot(left, right, preferred_element_type=F32)
            acc = term if acc is None else acc + term
        own = pl.ds(at + 2 * rows, size)
        value = same[0][own, :].astype(F32) + same[1][own, :].astype(F32)
        damp = jnp.concatenate(
            [
                jnp.broadcast_to(damp_ref[start + damp_at + j], (rows, W))
                for j in range(step)
            ],
            axis=0,
        )
        high, low = split(acc * (1.0 / shots) + damp * value)
        dst[0][pl.ds(at, size), :] = high
        dst[1][pl.ds(at, size), :] = low
        return carry

    lax.fori_loop(0, chunks, chunk, 0)


def kernel(
    n, nb, rows, shots,
    probes, illum, damp, wav, basis, r_out,
    p_left, p_right, l_left, l_right, d_left, d_right,
    xh, xl, rh, rl, yh, yl, zh, zl, fh, fl, ah, al,
    light, damps, g_own, g_all, halo_send, halo_recv, g_send, g_recv,
):
    me = lax.axis_index("mp")
    cells = nb * W

    barrier = pltpu.get_barrier_semaphore()

    def greet(d, carry):
        pl.semaphore_signal(
            barrier, inc=1, device_id={"mp": lax.rem(me + d, n)}, device_id_type=MESH
        )
        return carry

    lax.fori_loop(1, n, greet, 0)

    def put(b, value):
        high, low = split(value)
        xh[b * rows : (b + 1) * rows, :] = high
        xl[b * rows : (b + 1) * rows, :] = low

    for b in range(nb):
        put(b + 4, probes[:, b * W : (b + 1) * W])
        light[b + 3] = illum[:, b * W : (b + 1) * W]
        damps[b + 2] = damp[:, b * W : (b + 1) * W]

    pl.semaphore_wait(barrier, n - 1)

    def halo(src, depth, to_right, dst, slot):
        at = pl.ds(cells - depth * W, depth * W) if to_right else pl.ds(0, depth * W)
        peer = lax.rem(me + 1, n) if to_right else lax.rem(me + n - 1, n)
        return pltpu.make_async_remote_copy(
            src_ref=src.at[:, at], dst_ref=dst,
            send_sem=halo_send.at[slot], recv_sem=halo_recv.at[slot],
            device_id={"mp": peer}, device_id_type=MESH,
        )

    rightward = [halo(probes, 4, True, p_left, 0), halo(illum, 3, True, l_left, 1),
                 halo(damp, 2, True, d_left, 2)]
    leftward = [halo(probes, 4, False, p_right, 3), halo(illum, 3, False, l_right, 4),
                halo(damp, 2, False, d_right, 5)]

    @pl.when(me < n - 1)
    def _():
        for copy in rightward:
            copy.start()

    @pl.when(me > 0)
    def _():
        for copy in leftward:
            copy.start()

    taps = wav[...]
    halves = jnp.concatenate([taps[:, :W], taps[:, W : 2 * W]], axis=0)
    turn = jnp.where(iota((W, W), 0) + iota((W, W), 1) == W - 1, 1.0, 0.0)
    flipped = jnp.dot(halves, turn, precision=EXACT, preferred_element_type=F32)
    back = jnp.concatenate([flipped[shots:], flipped[:shots]], axis=1)
    back = pltpu.roll(back, 1, 1)
    final = taps[:, 2 * W : 2 * W + 1]
    back = jnp.where(iota((shots, 2 * W), 1) == 0, final, back)
    for s in range(shots):
        store_band(taps[s : s + 1, : 2 * W], final[s : s + 1], fh, fl, s)
        store_band(back[s : s + 1], taps[s : s + 1, 0:1], ah, al, s)

    @pl.when(me > 0)
    def _():
        for copy in rightward:
            copy.wait_recv()

    @pl.when(me == 0)
    def _():
        p_left[...] = jnp.zeros_like(p_left)
        l_left[...] = jnp.zeros_like(l_left)
        d_left[...] = jnp.zeros_like(d_left)

    @pl.when(me < n - 1)
    def _():
        for copy in leftward:
            copy.wait_recv()

    @pl.when(me == n - 1)
    def _():
        p_right[...] = jnp.zeros_like(p_right)
        l_right[...] = jnp.zeros_like(l_right)
        d_right[...] = jnp.zeros_like(d_right)

    for b in range(4):
        put(b, p_left[:, b * W : (b + 1) * W])
        put(nb + 4 + b, p_right[:, b * W : (b + 1) * W])
    for b in range(3):
        light[b] = l_left[:, b * W : (b + 1) * W]
        light[nb + 3 + b] = l_right[:, b * W : (b + 1) * W]
    for b in range(2):
        damps[b] = d_left[:, b * W : (b + 1) * W]
        damps[nb + 2 + b] = d_right[:, b * W : (b + 1) * W]

    def send_gram(k, packed):
        g_own[k] = packed
        g_all[k, me] = packed

        def send(d, carry):
            gram_copy(k, d).start()
            return carry

        lax.fori_loop(1, n, send, 0)

    def gram_copy(k, d):
        return pltpu.make_async_remote_copy(
            src_ref=g_own.at[k], dst_ref=g_all.at[k, me],
            send_sem=g_send.at[k, d], recv_sem=g_recv.at[k, me],
            device_id={"mp": lax.rem(me + d, n)}, device_id_type=MESH,
        )

    def gathered(k):
        def arrive(d, carry):
            peer = lax.rem(me + d, n)
            pltpu.make_async_remote_copy(
                src_ref=g_own.at[k], dst_ref=g_all.at[k, peer],
                send_sem=g_send.at[k, d], recv_sem=g_recv.at[k, peer],
                device_id={"mp": peer}, device_id_type=MESH,
            ).wait_recv()
            return carry

        lax.fori_loop(1, n, arrive, 0)
        return unpack(jnp.sum(g_all[k], axis=0)) / (n * cells)

    forward_stage(nb + 6, 2, rows, (xh, xl), (fh, fl), (rh, rl), light, 0, shots)
    adjoint_stage(nb + 4, 2, rows, (rh, rl), (ah, al), (yh, yl), (xh, xl), damps, 0, shots)

    @pl.when(me == 0)
    def _():
        for ref in (yh, yl):
            ref[: 2 * rows, :] = jnp.zeros((2 * rows, W), BF16)

    @pl.when(me == n - 1)
    def _():
        for ref in (yh, yl):
            ref[(nb + 2) * rows :, :] = jnp.zeros((2 * rows, W), BF16)

    send_gram(0, gram_of(yh, yl, 2 * rows, nb, rows))
    forward_stage(nb + 2, 2, rows, (yh, yl), (fh, fl), (rh, rl), light, 2, shots)
    adjoint_stage(nb, 2, rows, (rh, rl), (ah, al), (zh, zl), (yh, yl), damps, 2, shots)
    send_gram(1, gram_of(zh, zl, 0, nb, rows))

    _, inverse = factor(gathered(0), rows)
    second = gathered(1)[:, :rows]
    second = jnp.dot(inverse, second, precision=EXACT, preferred_element_type=F32)
    second = lax.dot_general(
        second, inverse, (((1,), (1,)), ((), ())), precision=EXACT, preferred_element_type=F32
    )
    second = jnp.concatenate([second, jnp.zeros((rows, LANES - rows), F32)], axis=1)
    lower, inverse_2 = factor(second, rows)
    r_out[...] = lower
    both = jnp.dot(inverse_2, inverse, precision=EXACT, preferred_element_type=F32)
    wide = jnp.concatenate([both] * 8, axis=1)
    tall = jnp.concatenate([wide] * 8, axis=0)
    group = 8 * rows
    same = iota((group, group), 0) // rows == iota((group, group), 1) // rows
    high, low = split(jnp.where(same, tall, 0.0))
    left = jnp.concatenate([high, high, low], axis=1)
    for g in range(nb // 8):
        at = slice(g * group, (g + 1) * group)
        right = jnp.concatenate([zh[at, :], zl[at, :], zh[at, :]], axis=0)
        out = jnp.dot(left, right, preferred_element_type=F32)
        for i in range(8):
            b = g * 8 + i
            basis[:, b * W : (b + 1) * W] = out[i * rows : (i + 1) * rows]

    @pl.when(me < n - 1)
    def _():
        for copy in rightward:
            copy.wait_send()

    @pl.when(me > 0)
    def _():
        for copy in leftward:
            copy.wait_send()

    def sent(d, carry):
        gram_copy(0, d).wait_send()
        gram_copy(1, d).wait_send()
        return carry

    lax.fori_loop(1, n, sent, 0)


def per_device(n, probes, illumination, damping, wavelets):
    rows, cells = probes.shape
    shots = illumination.shape[0]
    nb = cells // W
    damping = damping.reshape(1, cells)
    vmem = pltpu.VMEM
    scratch = [
        vmem((rows, 4 * W), F32), vmem((rows, 4 * W), F32),
        vmem((shots, 3 * W), F32), vmem((shots, 3 * W), F32),
        vmem((1, 2 * W), F32), vmem((1, 2 * W), F32),
    ]
    scratch += [vmem(((nb + 8) * rows, W), BF16)] * 2
    scratch += [vmem((shots, (nb + 6) * rows, W), BF16)] * 2
    scratch += [vmem(((nb + 4) * rows, W), BF16)] * 2
    scratch += [vmem((nb * rows, W), BF16)] * 2
    scratch += [vmem((shots, 3 * W, W), BF16)] * 4
    scratch += [
        vmem((nb + 6, shots, W), F32), vmem((nb + 4, 1, W), F32),
        vmem((2, 8, LANES), F32), vmem((2, n, 8, LANES), F32),
        pltpu.SemaphoreType.DMA((6,)), pltpu.SemaphoreType.DMA((6,)),
        pltpu.SemaphoreType.DMA((2, n)), pltpu.SemaphoreType.DMA((2, n)),
    ]
    return pl.pallas_call(
        functools.partial(kernel, n, nb, rows, shots),
        out_shape=(
            jax.ShapeDtypeStruct((rows, cells), F32),
            jax.ShapeDtypeStruct((rows, rows), F32),
        ),
        in_specs=[pl.BlockSpec(memory_space=vmem)] * 4,
        out_specs=(pl.BlockSpec(memory_space=vmem), pl.BlockSpec(memory_space=vmem)),
        scratch_shapes=scratch,
        compiler_params=pltpu.CompilerParams(
            collective_id=0, has_side_effects=True, vmem_limit_bytes=48 * 2**20
        ),
    )(probes, illumination, damping, wavelets)


def solution(mesh):
    in_specs = (
        P(None, ("parts", "mp")),
        P(None, ("parts", "mp")),
        P(("parts", "mp")),
        P("parts", None),
    )
    out_specs = (P(None, ("parts", "mp")), P("parts", None))
    return jax.shard_map(
        functools.partial(per_device, mesh.shape["mp"]),
        mesh=mesh, in_specs=in_specs, out_specs=out_specs, check_vma=False,
    )
```

```python
import functools

import jax
import jax.numpy as jnp
from jax import lax
from jax.experimental import pallas as pl
from jax.experimental.pallas import tpu as pltpu
from jax.sharding import PartitionSpec as P

W = 256
LANES = 128
MESH = pl.DeviceIdType.MESH
F32 = jnp.float32
BF16 = jnp.bfloat16
EXACT = lax.Precision.HIGHEST


def split(value):
    high = value.astype(BF16)
    return high, (value - high.astype(F32)).astype(BF16)


def iota(shape, dim):
    return lax.broadcasted_iota(jnp.int32, shape, dim)


def store_band(taps, last, high_ref, low_ref, shot):
    top = pltpu.roll(
        jnp.broadcast_to(taps, (LANES, 2 * W)), 0, 1, stride=1, stride_axis=0
    )
    bottom = jnp.concatenate([top[:, 2 * W - LANES :], top[:, : 2 * W - LANES]], axis=1)
    turned = jnp.concatenate([top, bottom], axis=0)
    edge = turned[:, :W]
    row, col = iota((W, W), 0), iota((W, W), 1)
    first = jnp.where(col < row, edge, jnp.where(col == row, last, 0.0))
    third = jnp.where(col >= row, edge, 0.0)
    for offset, tile in enumerate((first, turned[:, W:], third)):
        high, low = split(tile)
        rows = slice(offset * W, (offset + 1) * W)
        high_ref[shot, rows, :] = high
        low_ref[shot, rows, :] = low


def gram_of(high_ref, low_ref, start, block_count, rows):
    group = 8 * rows
    total = None
    for g in range(block_count // 8):
        at = slice(start + g * group, start + (g + 1) * group)
        high, low = high_ref[at, :], low_ref[at, :]
        left = jnp.concatenate([high, high, low], axis=1)
        right = jnp.concatenate([high, low, high], axis=1)
        term = lax.dot_general(
            left, right, (((1,), (1,)), ((), ())), preferred_element_type=F32
        )
        total = term if total is None else total + term
    same = iota((group, group), 0) // rows == iota((group, group), 1) // rows
    total = jnp.where(same, total, 0.0)
    folded = total[:rows]
    for i in range(1, 8):
        folded = folded + total[i * rows : (i + 1) * rows]
    folded = folded[:, :LANES] + folded[:, LANES:]
    folded = folded + pltpu.roll(folded, 64, 1)
    folded = folded + pltpu.roll(folded, 32, 1)
    lane = iota((8, LANES), 1) // 32
    packed = folded[:8]
    for i in range(1, 4):
        packed = jnp.where(lane == i, folded[8 * i : 8 * i + 8], packed)
    return packed


def unpack(packed):
    slabs = [packed] + [pltpu.roll(packed, LANES - 32 * i, 1) for i in range(1, 4)]
    return jnp.concatenate(slabs, axis=0)


def factor(gram, rows):
    row, lane = iota((rows, LANES), 0), iota((rows, LANES), 1)
    work = jnp.where(lane < rows, gram, jnp.where(lane == row + rows, 1.0, 0.0))
    unit = jnp.zeros((rows, LANES), F32)
    for k in range(rows):
        pivot_row = work[k : k + 1, :]
        ratio = work[:, k : k + 1] * (1.0 / work[k : k + 1, k : k + 1])
        unit = jnp.where((lane == k) & (row >= k), ratio, unit)
        work = work - jnp.where(row > k, ratio, 0.0) * pivot_row
    diagonal = jnp.where(lane == row, work, 0.0)
    down = jnp.sum(diagonal, axis=1, keepdims=True)
    along = jnp.sum(diagonal, axis=0, keepdims=True)
    lower = unit * jnp.sqrt(along)
    inverse = pltpu.roll(work, LANES - rows, 1) / jnp.sqrt(down)
    return lower[:, :rows], inverse[:, :rows]


def forward_blocks(starts, step, rows, src, weights, dst, light_ref, light_at, shots):
    size = step * rows
    ats = [s * rows if isinstance(s, int) else pl.multiple_of(s * rows, rows) for s in starts]

    def tall(ref, o):
        return jnp.concatenate([ref[pl.ds(at + o * rows, size), :] for at in ats], axis=0)

    highs = [tall(src[0], o) for o in range(3)]
    lows = [tall(src[1], o) for o in range(3)]
    left = jnp.concatenate(highs + lows + highs, axis=1)
    for s in range(shots):
        wh, wl = weights[0][s], weights[1][s]
        right = jnp.concatenate([wh, wh, wl], axis=0)
        acc = jnp.dot(left, right, preferred_element_type=F32)
        light = jnp.concatenate(
            [
                jnp.broadcast_to(light_ref[start + light_at + j, s : s + 1, :], (rows, W))
                for start in starts
                for j in range(step)
            ],
            axis=0,
        )
        high, low = split(acc * light)
        for i, at in enumerate(ats):
            dst[0][s, pl.ds(at, size), :] = high[i * size : (i + 1) * size]
            dst[1][s, pl.ds(at, size), :] = low[i * size : (i + 1) * size]


def forward_stage(first, count, chunks, *rest):
    step = count // chunks

    def chunk(c, carry):
        forward_blocks([first + c * step], step, *rest)
        return carry

    lax.fori_loop(0, chunks, chunk, 0)


def adjoint_stage(count, chunks, rows, src, weights, dst, same, damp_ref, damp_at, shots):
    step = count // chunks
    size = step * rows

    def chunk(c, carry):
        start = c * step
        at = pl.multiple_of(start * rows, rows)
        acc = None
        for s in range(shots):
            highs = [src[0][s, pl.ds(at + o * rows, size), :] for o in range(3)]
            lows = [src[1][s, pl.ds(at + o * rows, size), :] for o in range(3)]
            wh, wl = weights[0][s], weights[1][s]
            left = jnp.concatenate(highs + lows + highs, axis=1)
            right = jnp.concatenate([wh, wh, wl], axis=0)
            term = jnp.dot(left, right, preferred_element_type=F32)
            acc = term if acc is None else acc + term
        own = pl.ds(at + 2 * rows, size)
        value = same[0][own, :].astype(F32) + same[1][own, :].astype(F32)
        damp = jnp.concatenate(
            [
                jnp.broadcast_to(damp_ref[start + damp_at + j], (rows, W))
                for j in range(step)
            ],
            axis=0,
        )
        high, low = split(acc * (1.0 / shots) + damp * value)
        dst[0][pl.ds(at, size), :] = high
        dst[1][pl.ds(at, size), :] = low
        return carry

    lax.fori_loop(0, chunks, chunk, 0)


def kernel(
    n, nb, rows, shots,
    probes_in, illum_in, damp_in, wav_in, basis, r_out,
    probes, illum, damp, wav, in_sems,
    p_left, p_right, l_left, l_right, d_left, d_right,
    xh, xl, rh, rl, yh, yl, zh, zl, fh, fl, ah, al,
    light, damps, g_own, g_all, halo_send, halo_recv, g_send, g_recv,
):
    me = lax.axis_index("mp")
    cells = nb * W

    loads = [
        pltpu.make_async_copy(src, dst, in_sems.at[i])
        for i, (src, dst) in enumerate(
            ((wav_in, wav), (probes_in, probes), (illum_in, illum), (damp_in, damp))
        )
    ]
    for load in loads:
        load.start()

    barrier = pltpu.get_barrier_semaphore()

    def greet(d, carry):
        pl.semaphore_signal(
            barrier, inc=1, device_id={"mp": lax.rem(me + d, n)}, device_id_type=MESH
        )
        return carry

    lax.fori_loop(1, n, greet, 0)

    loads[0].wait()
    taps = wav[...]
    halves = jnp.concatenate([taps[:, :W], taps[:, W : 2 * W]], axis=0)
    turn = jnp.where(iota((W, W), 0) + iota((W, W), 1) == W - 1, 1.0, 0.0)
    flipped = jnp.dot(halves, turn, precision=EXACT, preferred_element_type=F32)
    back = jnp.concatenate([flipped[shots:], flipped[:shots]], axis=1)
    back = pltpu.roll(back, 1, 1)
    final = taps[:, 2 * W : 2 * W + 1]
    back = jnp.where(iota((shots, 2 * W), 1) == 0, final, back)
    for s in range(shots):
        store_band(taps[s : s + 1, : 2 * W], final[s : s + 1], fh, fl, s)
        store_band(back[s : s + 1], taps[s : s + 1, 0:1], ah, al, s)

    pl.semaphore_wait(barrier, n - 1)

    def halo(src, depth, to_right, dst, slot):
        at = pl.ds(cells - depth * W, depth * W) if to_right else pl.ds(0, depth * W)
        peer = lax.rem(me + 1, n) if to_right else lax.rem(me + n - 1, n)
        return pltpu.make_async_remote_copy(
            src_ref=src.at[:, at], dst_ref=dst,
            send_sem=halo_send.at[slot], recv_sem=halo_recv.at[slot],
            device_id={"mp": peer}, device_id_type=MESH,
        )

    rightward = [halo(probes_in, 4, True, p_left, 0), halo(illum_in, 3, True, l_left, 1),
                 halo(damp_in, 2, True, d_left, 2)]
    leftward = [halo(probes_in, 4, False, p_right, 3), halo(illum_in, 3, False, l_right, 4),
                halo(damp_in, 2, False, d_right, 5)]

    @pl.when(me < n - 1)
    def _():
        for copy in rightward:
            copy.start()

    @pl.when(me > 0)
    def _():
        for copy in leftward:
            copy.start()

    def put(b, value):
        high, low = split(value)
        xh[b * rows : (b + 1) * rows, :] = high
        xl[b * rows : (b + 1) * rows, :] = low

    for load in loads[1:]:
        load.wait()
    for b in range(nb):
        put(b + 4, probes[:, b * W : (b + 1) * W])
        light[b + 3] = illum[:, b * W : (b + 1) * W]
        damps[b + 2] = damp[:, b * W : (b + 1) * W]

    forward = (rows, (xh, xl), (fh, fl), (rh, rl), light, 0, shots)
    forward_stage(4, nb - 2, 2, *forward)

    @pl.when(me > 0)
    def _():
        for copy in rightward:
            copy.wait_recv()

    @pl.when(me == 0)
    def _():
        p_left[...] = jnp.zeros_like(p_left)
        l_left[...] = jnp.zeros_like(l_left)
        d_left[...] = jnp.zeros_like(d_left)

    @pl.when(me < n - 1)
    def _():
        for copy in leftward:
            copy.wait_recv()

    @pl.when(me == n - 1)
    def _():
        p_right[...] = jnp.zeros_like(p_right)
        l_right[...] = jnp.zeros_like(l_right)
        d_right[...] = jnp.zeros_like(d_right)

    for b in range(4):
        put(b, p_left[:, b * W : (b + 1) * W])
        put(nb + 4 + b, p_right[:, b * W : (b + 1) * W])
    for b in range(3):
        light[b] = l_left[:, b * W : (b + 1) * W]
        light[nb + 3 + b] = l_right[:, b * W : (b + 1) * W]
    for b in range(2):
        damps[b] = d_left[:, b * W : (b + 1) * W]
        damps[nb + 2 + b] = d_right[:, b * W : (b + 1) * W]

    def send_gram(k, packed):
        g_own[k] = packed
        g_all[k, me] = packed

        def send(d, carry):
            gram_copy(k, d).start()
            return carry

        lax.fori_loop(1, n, send, 0)

    def gram_copy(k, d):
        return pltpu.make_async_remote_copy(
            src_ref=g_own.at[k], dst_ref=g_all.at[k, me],
            send_sem=g_send.at[k, d], recv_sem=g_recv.at[k, me],
            device_id={"mp": lax.rem(me + d, n)}, device_id_type=MESH,
        )

    def gathered(k):
        def arrive(d, carry):
            peer = lax.rem(me + d, n)
            pltpu.make_async_remote_copy(
                src_ref=g_own.at[k], dst_ref=g_all.at[k, peer],
                send_sem=g_send.at[k, d], recv_sem=g_recv.at[k, peer],
                device_id={"mp": peer}, device_id_type=MESH,
            ).wait_recv()
            return carry

        lax.fori_loop(1, n, arrive, 0)
        return unpack(jnp.sum(g_all[k], axis=0)) / (n * cells)

    forward_blocks([0, nb + 2], 4, *forward)
    adjoint_stage(nb + 4, 2, rows, (rh, rl), (ah, al), (yh, yl), (xh, xl), damps, 0, shots)

    @pl.when(me == 0)
    def _():
        for ref in (yh, yl):
            ref[: 2 * rows, :] = jnp.zeros((2 * rows, W), BF16)

    @pl.when(me == n - 1)
    def _():
        for ref in (yh, yl):
            ref[(nb + 2) * rows :, :] = jnp.zeros((2 * rows, W), BF16)

    send_gram(0, gram_of(yh, yl, 2 * rows, nb, rows))
    forward_stage(0, nb + 2, 2, rows, (yh, yl), (fh, fl), (rh, rl), light, 2, shots)
    adjoint_stage(nb, 2, rows, (rh, rl), (ah, al), (zh, zl), (yh, yl), damps, 2, shots)
    send_gram(1, gram_of(zh, zl, 0, nb, rows))

    _, inverse = factor(gathered(0), rows)
    second = gathered(1)[:, :rows]
    second = jnp.dot(inverse, second, precision=EXACT, preferred_element_type=F32)
    second = lax.dot_general(
        second, inverse, (((1,), (1,)), ((), ())), precision=EXACT, preferred_element_type=F32
    )
    second = jnp.concatenate([second, jnp.zeros((rows, LANES - rows), F32)], axis=1)
    lower, inverse_2 = factor(second, rows)
    r_out[...] = lower
    both = jnp.dot(inverse_2, inverse, precision=EXACT, preferred_element_type=F32)
    wide = jnp.concatenate([both] * 8, axis=1)
    tall = jnp.concatenate([wide] * 8, axis=0)
    group = 8 * rows
    same = iota((group, group), 0) // rows == iota((group, group), 1) // rows
    high, low = split(jnp.where(same, tall, 0.0))
    left = jnp.concatenate([high, high, low], axis=1)
    for g in range(nb // 8):
        at = slice(g * group, (g + 1) * group)
        right = jnp.concatenate([zh[at, :], zl[at, :], zh[at, :]], axis=0)
        out = jnp.dot(left, right, preferred_element_type=F32)
        for i in range(8):
            b = g * 8 + i
            basis[:, b * W : (b + 1) * W] = out[i * rows : (i + 1) * rows]

    @pl.when(me < n - 1)
    def _():
        for copy in rightward:
            copy.wait_send()

    @pl.when(me > 0)
    def _():
        for copy in leftward:
            copy.wait_send()

    def sent(d, carry):
        gram_copy(0, d).wait_send()
        gram_copy(1, d).wait_send()
        return carry

    lax.fori_loop(1, n, sent, 0)


def per_device(n, probes, illumination, damping, wavelets):
    rows, cells = probes.shape
    shots = illumination.shape[0]
    nb = cells // W
    damping = damping.reshape(1, cells)
    vmem = pltpu.VMEM
    scratch = [
        vmem((rows, cells), F32), vmem((shots, cells), F32), vmem((1, cells), F32),
        vmem(wavelets.shape, F32), pltpu.SemaphoreType.DMA((4,)),
        vmem((rows, 4 * W), F32), vmem((rows, 4 * W), F32),
        vmem((shots, 3 * W), F32), vmem((shots, 3 * W), F32),
        vmem((1, 2 * W), F32), vmem((1, 2 * W), F32),
    ]
    scratch += [vmem(((nb + 8) * rows, W), BF16)] * 2
    scratch += [vmem((shots, (nb + 6) * rows, W), BF16)] * 2
    scratch += [vmem(((nb + 4) * rows, W), BF16)] * 2
    scratch += [vmem((nb * rows, W), BF16)] * 2
    scratch += [vmem((shots, 3 * W, W), BF16)] * 4
    scratch += [
        vmem((nb + 6, shots, W), F32), vmem((nb + 4, 1, W), F32),
        vmem((2, 8, LANES), F32), vmem((2, n, 8, LANES), F32),
        pltpu.SemaphoreType.DMA((6,)), pltpu.SemaphoreType.DMA((6,)),
        pltpu.SemaphoreType.DMA((2, n)), pltpu.SemaphoreType.DMA((2, n)),
    ]
    return pl.pallas_call(
        functools.partial(kernel, n, nb, rows, shots),
        out_shape=(
            jax.ShapeDtypeStruct((rows, cells), F32),
            jax.ShapeDtypeStruct((rows, rows), F32),
        ),
        in_specs=[pl.BlockSpec(memory_space=pltpu.HBM)] * 4,
        out_specs=(pl.BlockSpec(memory_space=vmem), pl.BlockSpec(memory_space=vmem)),
        scratch_shapes=scratch,
        compiler_params=pltpu.CompilerParams(
            collective_id=0, has_side_effects=True, vmem_limit_bytes=60 * 2**20
        ),
    )(probes, illumination, damping, wavelets)


def solution(mesh):
    in_specs = (
        P(None, ("parts", "mp")),
        P(None, ("parts", "mp")),
        P(("parts", "mp")),
        P("parts", None),
    )
    out_specs = (P(None, ("parts", "mp")), P("parts", None))
    return jax.shard_map(
        functools.partial(per_device, mesh.shape["mp"]),
        mesh=mesh, in_specs=in_specs, out_specs=out_specs, check_vma=False,
    )
```

```python
import functools

import jax
import jax.numpy as jnp
from jax import lax
from jax.experimental import pallas as pl
from jax.experimental.pallas import tpu as pltpu
from jax.sharding import PartitionSpec as P

W = 256
LANES = 128
MESH = pl.DeviceIdType.MESH
F32 = jnp.float32
BF16 = jnp.bfloat16
EXACT = lax.Precision.HIGHEST


def split(value):
    high = value.astype(BF16)
    return high, (value - high.astype(F32)).astype(BF16)


def iota(shape, dim):
    return lax.broadcasted_iota(jnp.int32, shape, dim)


def store_band(taps, last, high_ref, low_ref, shot):
    top = pltpu.roll(
        jnp.broadcast_to(taps, (LANES, 2 * W)), 0, 1, stride=1, stride_axis=0
    )
    bottom = jnp.concatenate([top[:, 2 * W - LANES :], top[:, : 2 * W - LANES]], axis=1)
    turned = jnp.concatenate([top, bottom], axis=0)
    edge = turned[:, :W]
    row, col = iota((W, W), 0), iota((W, W), 1)
    first = jnp.where(col < row, edge, jnp.where(col == row, last, 0.0))
    third = jnp.where(col >= row, edge, 0.0)
    for offset, tile in enumerate((first, turned[:, W:], third)):
        high, low = split(tile)
        rows = slice(offset * W, (offset + 1) * W)
        high_ref[shot, rows, :] = high
        low_ref[shot, rows, :] = low


def gram_of(high_ref, low_ref, start, block_count, rows):
    group = 8 * rows
    total = None
    for g in range(block_count // 8):
        at = slice(start + g * group, start + (g + 1) * group)
        high, low = high_ref[at, :], low_ref[at, :]
        left = jnp.concatenate([high, high, low], axis=1)
        right = jnp.concatenate([high, low, high], axis=1)
        term = lax.dot_general(
            left, right, (((1,), (1,)), ((), ())), preferred_element_type=F32
        )
        total = term if total is None else total + term
    same = iota((group, group), 0) // rows == iota((group, group), 1) // rows
    total = jnp.where(same, total, 0.0)
    folded = total[:rows]
    for i in range(1, 8):
        folded = folded + total[i * rows : (i + 1) * rows]
    folded = folded[:, :LANES] + folded[:, LANES:]
    folded = folded + pltpu.roll(folded, 64, 1)
    folded = folded + pltpu.roll(folded, 32, 1)
    lane = iota((8, LANES), 1) // 32
    packed = folded[:8]
    for i in range(1, 4):
        packed = jnp.where(lane == i, folded[8 * i : 8 * i + 8], packed)
    return packed


def unpack(packed):
    slabs = [packed] + [pltpu.roll(packed, LANES - 32 * i, 1) for i in range(1, 4)]
    return jnp.concatenate(slabs, axis=0)


def factor(gram, rows):
    row, lane = iota((rows, LANES), 0), iota((rows, LANES), 1)
    work = jnp.where(lane < rows, gram, jnp.where(lane == row + rows, 1.0, 0.0))
    unit = jnp.zeros((rows, LANES), F32)
    for k in range(rows):
        pivot_row = work[k : k + 1, :]
        ratio = work[:, k : k + 1] * (1.0 / work[k : k + 1, k : k + 1])
        unit = jnp.where((lane == k) & (row >= k), ratio, unit)
        work = work - jnp.where(row > k, ratio, 0.0) * pivot_row
    diagonal = jnp.where(lane == row, work, 0.0)
    down = jnp.sum(diagonal, axis=1, keepdims=True)
    along = jnp.sum(diagonal, axis=0, keepdims=True)
    lower = unit * jnp.sqrt(along)
    inverse = pltpu.roll(work, LANES - rows, 1) / jnp.sqrt(down)
    return lower[:, :rows], inverse[:, :rows]


def forward_blocks(starts, step, rows, src, weights, dst, light_ref, light_at, shots):
    size = step * rows
    ats = [s * rows if isinstance(s, int) else pl.multiple_of(s * rows, rows) for s in starts]

    def tall(ref, o):
        return jnp.concatenate([ref[pl.ds(at + o * rows, size), :] for at in ats], axis=0)

    highs = [tall(src[0], o) for o in range(3)]
    lows = [tall(src[1], o) for o in range(3)]
    left = jnp.concatenate(highs + lows + highs, axis=1)
    for s in range(shots):
        wh, wl = weights[0][s], weights[1][s]
        right = jnp.concatenate([wh, wh, wl], axis=0)
        acc = jnp.dot(left, right, preferred_element_type=F32)
        light = jnp.concatenate(
            [
                jnp.broadcast_to(light_ref[start + light_at + j, s : s + 1, :], (rows, W))
                for start in starts
                for j in range(step)
            ],
            axis=0,
        )
        high, low = split(acc * light)
        for i, at in enumerate(ats):
            dst[0][s, pl.ds(at, size), :] = high[i * size : (i + 1) * size]
            dst[1][s, pl.ds(at, size), :] = low[i * size : (i + 1) * size]


def forward_stage(first, count, chunks, *rest):
    step = count // chunks

    def chunk(c, carry):
        forward_blocks([first + c * step], step, *rest)
        return carry

    lax.fori_loop(0, chunks, chunk, 0)


def adjoint_stage(count, chunks, rows, src, weights, dst, same, damp_ref, damp_at, shots):
    step = count // chunks
    size = step * rows

    def chunk(c, carry):
        start = c * step
        at = pl.multiple_of(start * rows, rows)
        left, right = [], []
        for s in range(shots):
            highs = [src[0][s, pl.ds(at + o * rows, size), :] for o in range(3)]
            lows = [src[1][s, pl.ds(at + o * rows, size), :] for o in range(3)]
            wh, wl = weights[0][s], weights[1][s]
            left += highs + lows + highs
            right += [wh, wh, wl]
        acc = jnp.dot(
            jnp.concatenate(left, axis=1),
            jnp.concatenate(right, axis=0),
            preferred_element_type=F32,
        )
        own = pl.ds(at + 2 * rows, size)
        value = same[0][own, :].astype(F32) + same[1][own, :].astype(F32)
        damp = jnp.concatenate(
            [
                jnp.broadcast_to(damp_ref[start + damp_at + j], (rows, W))
                for j in range(step)
            ],
            axis=0,
        )
        high, low = split(acc * (1.0 / shots) + damp * value)
        dst[0][pl.ds(at, size), :] = high
        dst[1][pl.ds(at, size), :] = low
        return carry

    lax.fori_loop(0, chunks, chunk, 0)


def kernel(
    n, nb, rows, shots,
    probes_in, illum_in, damp_in, wav_in, basis, r_out,
    probes, illum, damp, wav, in_sems,
    p_left, p_right, l_left, l_right, d_left, d_right,
    xh, xl, rh, rl, yh, yl, zh, zl, fh, fl, ah, al,
    light, damps, g_own, g_all, halo_send, halo_recv, g_send, g_recv,
):
    me = lax.axis_index("mp")
    cells = nb * W

    loads = [
        pltpu.make_async_copy(src, dst, in_sems.at[i])
        for i, (src, dst) in enumerate(
            ((wav_in, wav), (probes_in, probes), (illum_in, illum), (damp_in, damp))
        )
    ]
    for load in loads:
        load.start()

    barrier = pltpu.get_barrier_semaphore()

    def greet(d, carry):
        pl.semaphore_signal(
            barrier, inc=1, device_id={"mp": lax.rem(me + d, n)}, device_id_type=MESH
        )
        return carry

    lax.fori_loop(1, n, greet, 0)

    loads[0].wait()
    taps = wav[...]
    halves = jnp.concatenate([taps[:, :W], taps[:, W : 2 * W]], axis=0)
    turn = jnp.where(iota((W, W), 0) + iota((W, W), 1) == W - 1, 1.0, 0.0)
    flipped = jnp.dot(halves, turn, precision=EXACT, preferred_element_type=F32)
    back = jnp.concatenate([flipped[shots:], flipped[:shots]], axis=1)
    back = pltpu.roll(back, 1, 1)
    final = taps[:, 2 * W : 2 * W + 1]
    back = jnp.where(iota((shots, 2 * W), 1) == 0, final, back)
    for s in range(shots):
        store_band(taps[s : s + 1, : 2 * W], final[s : s + 1], fh, fl, s)
        store_band(back[s : s + 1], taps[s : s + 1, 0:1], ah, al, s)

    pl.semaphore_wait(barrier, n - 1)

    def halo(src, depth, to_right, dst, slot):
        at = pl.ds(cells - depth * W, depth * W) if to_right else pl.ds(0, depth * W)
        peer = lax.rem(me + 1, n) if to_right else lax.rem(me + n - 1, n)
        return pltpu.make_async_remote_copy(
            src_ref=src.at[:, at], dst_ref=dst,
            send_sem=halo_send.at[slot], recv_sem=halo_recv.at[slot],
            device_id={"mp": peer}, device_id_type=MESH,
        )

    rightward = [halo(probes_in, 4, True, p_left, 0), halo(illum_in, 3, True, l_left, 1),
                 halo(damp_in, 2, True, d_left, 2)]
    leftward = [halo(probes_in, 4, False, p_right, 3), halo(illum_in, 3, False, l_right, 4),
                halo(damp_in, 2, False, d_right, 5)]

    @pl.when(me < n - 1)
    def _():
        for copy in rightward:
            copy.start()

    @pl.when(me > 0)
    def _():
        for copy in leftward:
            copy.start()

    def put(b, value):
        high, low = split(value)
        xh[b * rows : (b + 1) * rows, :] = high
        xl[b * rows : (b + 1) * rows, :] = low

    for load in loads[1:]:
        load.wait()
    for b in range(nb):
        put(b + 4, probes[:, b * W : (b + 1) * W])
        light[b + 3] = illum[:, b * W : (b + 1) * W]
        damps[b + 2] = damp[:, b * W : (b + 1) * W]

    forward = (rows, (xh, xl), (fh, fl), (rh, rl), light, 0, shots)
    forward_stage(4, nb - 2, 2, *forward)

    @pl.when(me > 0)
    def _():
        for copy in rightward:
            copy.wait_recv()

    @pl.when(me == 0)
    def _():
        p_left[...] = jnp.zeros_like(p_left)
        l_left[...] = jnp.zeros_like(l_left)
        d_left[...] = jnp.zeros_like(d_left)

    @pl.when(me < n - 1)
    def _():
        for copy in leftward:
            copy.wait_recv()

    @pl.when(me == n - 1)
    def _():
        p_right[...] = jnp.zeros_like(p_right)
        l_right[...] = jnp.zeros_like(l_right)
        d_right[...] = jnp.zeros_like(d_right)

    for b in range(4):
        put(b, p_left[:, b * W : (b + 1) * W])
        put(nb + 4 + b, p_right[:, b * W : (b + 1) * W])
    for b in range(3):
        light[b] = l_left[:, b * W : (b + 1) * W]
        light[nb + 3 + b] = l_right[:, b * W : (b + 1) * W]
    for b in range(2):
        damps[b] = d_left[:, b * W : (b + 1) * W]
        damps[nb + 2 + b] = d_right[:, b * W : (b + 1) * W]

    def send_gram(k, packed):
        g_own[k] = packed
        g_all[k, me] = packed

        def send(d, carry):
            gram_copy(k, d).start()
            return carry

        lax.fori_loop(1, n, send, 0)

    def gram_copy(k, d):
        return pltpu.make_async_remote_copy(
            src_ref=g_own.at[k], dst_ref=g_all.at[k, me],
            send_sem=g_send.at[k, d], recv_sem=g_recv.at[k, me],
            device_id={"mp": lax.rem(me + d, n)}, device_id_type=MESH,
        )

    def gathered(k):
        def arrive(d, carry):
            peer = lax.rem(me + d, n)
            pltpu.make_async_remote_copy(
                src_ref=g_own.at[k], dst_ref=g_all.at[k, peer],
                send_sem=g_send.at[k, d], recv_sem=g_recv.at[k, peer],
                device_id={"mp": peer}, device_id_type=MESH,
            ).wait_recv()
            return carry

        lax.fori_loop(1, n, arrive, 0)
        return unpack(jnp.sum(g_all[k], axis=0)) / (n * cells)

    forward_blocks([0, nb + 2], 4, *forward)
    adjoint_stage(nb + 4, 2, rows, (rh, rl), (ah, al), (yh, yl), (xh, xl), damps, 0, shots)

    @pl.when(me == 0)
    def _():
        for ref in (yh, yl):
            ref[: 2 * rows, :] = jnp.zeros((2 * rows, W), BF16)

    @pl.when(me == n - 1)
    def _():
        for ref in (yh, yl):
            ref[(nb + 2) * rows :, :] = jnp.zeros((2 * rows, W), BF16)

    send_gram(0, gram_of(yh, yl, 2 * rows, nb, rows))
    forward_stage(0, nb + 2, 2, rows, (yh, yl), (fh, fl), (rh, rl), light, 2, shots)
    adjoint_stage(nb, 2, rows, (rh, rl), (ah, al), (zh, zl), (yh, yl), damps, 2, shots)
    send_gram(1, gram_of(zh, zl, 0, nb, rows))

    _, inverse = factor(gathered(0), rows)
    second = gathered(1)[:, :rows]
    second = jnp.dot(inverse, second, precision=EXACT, preferred_element_type=F32)
    second = lax.dot_general(
        second, inverse, (((1,), (1,)), ((), ())), precision=EXACT, preferred_element_type=F32
    )
    second = jnp.concatenate([second, jnp.zeros((rows, LANES - rows), F32)], axis=1)
    lower, inverse_2 = factor(second, rows)
    r_out[...] = lower
    both = jnp.dot(inverse_2, inverse, precision=EXACT, preferred_element_type=F32)
    wide = jnp.concatenate([both] * 8, axis=1)
    tall = jnp.concatenate([wide] * 8, axis=0)
    group = 8 * rows
    same = iota((group, group), 0) // rows == iota((group, group), 1) // rows
    high, low = split(jnp.where(same, tall, 0.0))
    left = jnp.concatenate([high, high, low], axis=1)
    for g in range(nb // 8):
        at = slice(g * group, (g + 1) * group)
        right = jnp.concatenate([zh[at, :], zl[at, :], zh[at, :]], axis=0)
        out = jnp.dot(left, right, preferred_element_type=F32)
        for i in range(8):
            b = g * 8 + i
            basis[:, b * W : (b + 1) * W] = out[i * rows : (i + 1) * rows]

    @pl.when(me < n - 1)
    def _():
        for copy in rightward:
            copy.wait_send()

    @pl.when(me > 0)
    def _():
        for copy in leftward:
            copy.wait_send()

    def sent(d, carry):
        gram_copy(0, d).wait_send()
        gram_copy(1, d).wait_send()
        return carry

    lax.fori_loop(1, n, sent, 0)


def per_device(n, probes, illumination, damping, wavelets):
    rows, cells = probes.shape
    shots = illumination.shape[0]
    nb = cells // W
    damping = damping.reshape(1, cells)
    vmem = pltpu.VMEM
    scratch = [
        vmem((rows, cells), F32), vmem((shots, cells), F32), vmem((1, cells), F32),
        vmem(wavelets.shape, F32), pltpu.SemaphoreType.DMA((4,)),
        vmem((rows, 4 * W), F32), vmem((rows, 4 * W), F32),
        vmem((shots, 3 * W), F32), vmem((shots, 3 * W), F32),
        vmem((1, 2 * W), F32), vmem((1, 2 * W), F32),
    ]
    scratch += [vmem(((nb + 8) * rows, W), BF16)] * 2
    scratch += [vmem((shots, (nb + 6) * rows, W), BF16)] * 2
    scratch += [vmem(((nb + 4) * rows, W), BF16)] * 2
    scratch += [vmem((nb * rows, W), BF16)] * 2
    scratch += [vmem((shots, 3 * W, W), BF16)] * 4
    scratch += [
        vmem((nb + 6, shots, W), F32), vmem((nb + 4, 1, W), F32),
        vmem((2, 8, LANES), F32), vmem((2, n, 8, LANES), F32),
        pltpu.SemaphoreType.DMA((6,)), pltpu.SemaphoreType.DMA((6,)),
        pltpu.SemaphoreType.DMA((2, n)), pltpu.SemaphoreType.DMA((2, n)),
    ]
    return pl.pallas_call(
        functools.partial(kernel, n, nb, rows, shots),
        out_shape=(
            jax.ShapeDtypeStruct((rows, cells), F32),
            jax.ShapeDtypeStruct((rows, rows), F32),
        ),
        in_specs=[pl.BlockSpec(memory_space=pltpu.HBM)] * 4,
        out_specs=(pl.BlockSpec(memory_space=vmem), pl.BlockSpec(memory_space=vmem)),
        scratch_shapes=scratch,
        compiler_params=pltpu.CompilerParams(
            collective_id=0, has_side_effects=True, vmem_limit_bytes=60 * 2**20
        ),
    )(probes, illumination, damping, wavelets)


def solution(mesh):
    in_specs = (
        P(None, ("parts", "mp")),
        P(None, ("parts", "mp")),
        P(("parts", "mp")),
        P("parts", None),
    )
    out_specs = (P(None, ("parts", "mp")), P("parts", None))
    return jax.shard_map(
        functools.partial(per_device, mesh.shape["mp"]),
        mesh=mesh, in_specs=in_specs, out_specs=out_specs, check_vma=False,
    )
```
